32 devices in a mesh: ctx: 16 (over z, y, core), head: 2 (over x).
Axes of the slice: x: 2, y: 2, z: 4, core: 2. Of those that a mesh axis runs over, the one named last changes fastest.
Arguments:
- queries: bfloat16 [8192, 4096], P('ctx', 'head'), may hold values from -48 to 48
- keys: bfloat16 [8192, 1024], P('ctx', 'head'), may hold values from -4 to 4
- values: bfloat16 [8192, 1024], P('ctx', 'head'), may hold values from -6 to 6
- doc_start: int32 [8192], P('ctx'), may hold values from 0 to 8191, as said below
- out_weight: bfloat16 [4096, 4096], P('head'), may hold values from -0.09375 to 0.09375
Outputs:
- mixed: bfloat16 [8192, 4096], P(('ctx', 'head'))
The draws below stay inside these ranges and needn't reach their ends.
Inputs may be any that keep to these rules, and one draw needn't show every extreme that they name: doc_start is non-decreasing, doc_start[i] <= i, and all tokens of a document share its first position; every document has at most 4096 tokens and one document has exactly 4096; the 4096-token document starts at a multiple of 1024, and all other documents lie inside aligned cells of 1024 tokens.
All inputs are finite; a program needn't handle non-finite values.
Results may differ from the reference program's by a relative error of at most 0.015.
Values may be sent and summed in bfloat16 or wider, within the bound.
A program may use at most 448 MiB of HBM per device.

```python
import jax
import jax.numpy as jnp
from jax import lax

D = 4096
QH = 32
KVH = 8
HD = 128
GROUP = 4
TOK_DEV = 512
SHORT = 1024
TOKENS = 8192
LONGEST = 4096
N_CTX = 16


def query_key_pair(key):
    key_part = jnp.clip(jax.random.normal(jax.random.fold_in(key, 11), (TOKENS, KVH, HD), jnp.float32), -4.0, 4.0)
    query_part = jnp.clip(jax.random.normal(jax.random.fold_in(key, 12), (TOKENS, KVH, GROUP, HD), jnp.float32), -4.0, 4.0)
    return (key_part, query_part)


def draw_queries(key, part):
    key_part, query_part = query_key_pair(key)
    return query_part.reshape(TOKENS, QH * HD).astype(jnp.bfloat16)


def draw_keys(key, part):
    key_part, query_part = query_key_pair(key)
    return key_part.reshape(TOKENS, KVH * HD).astype(jnp.bfloat16)


def draw_doc_start(key, part):
    cells = TOKENS // SHORT
    split = jax.random.randint(jax.random.fold_in(key, 21), (cells,), 1, SHORT + 1)
    long_start = jax.random.randint(jax.random.fold_in(key, 22), (), 0, (TOKENS - LONGEST) // SHORT + 1) * SHORT
    position = jnp.arange(TOKENS, dtype=jnp.int32)
    cell_index = position // SHORT
    base = cell_index * SHORT
    cut = split[cell_index]
    short_start = jnp.where(position - base < cut, base, base + cut)
    inside = (position >= long_start) & (position < long_start + LONGEST)
    return jnp.where(inside, long_start, short_start).astype(jnp.int32)


def levels(rng, dims, cuts, low, high):
    loudness = 1.0
    for dim, parts in cuts:
        draws = jax.random.uniform(jax.random.fold_in(jax.random.fold_in(rng, 6), dim), (parts,), jnp.float32, low / len(cuts), high / len(cuts))
        loudness = loudness * jnp.repeat(jnp.exp(draws), dims[dim] // parts).reshape((-1,) + (1,) * (len(dims) - 1 - dim))
    return loudness


def noise(key, extent, spread, limit, shards=(), held_as=jnp.bfloat16):
    values = jax.random.normal(key, extent, jnp.float32) * spread
    if len(shards) > 0:
        values = levels(key, extent, shards, -0.22, 0.18) * values
    return jnp.clip(values, min=-limit, max=limit).astype(held_as)


def setup_inputs(seed: int = 0) -> dict:
    arg_keys = jax.random.split(jax.random.key(seed), 6)
    return {
        "queries": draw_queries(jax.random.fold_in(arg_keys[5], 71), 0),
        "keys": draw_keys(jax.random.fold_in(arg_keys[5], 71), 0),
        "values": noise(arg_keys[2], (TOKENS, KVH * HD), 1.0, 6.0, ((0, 16), (1, 2))),
        "doc_start": draw_doc_start(jax.random.fold_in(arg_keys[5], 71), 0),
        "out_weight": noise(arg_keys[4], (QH * HD, D), (QH * HD) ** -0.5, 0.09375, ((0, 2),)),
    }


NEG_FILL = -1.0e30


def reference(queries, keys, values, doc_start, out_weight):
    front = LONGEST
    width = front + TOK_DEV
    keys_pad = jnp.pad(keys, ((front, 0), (0, 0)))
    values_pad = jnp.pad(values, ((front, 0), (0, 0)))

    def one_block(index):
        start = (index * TOK_DEV).astype(jnp.int32)
        query_blk = lax.dynamic_slice_in_dim(queries, start, TOK_DEV, 0).astype(jnp.float32).reshape(TOK_DEV, KVH, GROUP, HD)
        key_blk = lax.dynamic_slice_in_dim(keys_pad, start, width, 0).astype(jnp.float32).reshape(width, KVH, HD)
        value_blk = lax.dynamic_slice_in_dim(values_pad, start, width, 0).astype(jnp.float32).reshape(width, KVH, HD)
        doc_rows = lax.dynamic_slice_in_dim(doc_start, start, TOK_DEV, 0)
        query_pos = start + jnp.arange(TOK_DEV, dtype=jnp.int32)
        key_pos = start - front + jnp.arange(width, dtype=jnp.int32)
        allowed = (key_pos[None, :] >= doc_rows[:, None]) & (key_pos[None, :] <= query_pos[:, None])
        scores = jnp.einsum("tkgd,skd->kgts", query_blk, key_blk, precision=lax.Precision.HIGHEST) * (HD ** -0.5)
        scores = jnp.where(allowed, scores, NEG_FILL)
        top = jnp.max(scores, axis=-1)
        weights = jnp.where(allowed, jnp.exp(scores - top[..., None]), 0.0)
        total = jnp.sum(weights, axis=-1)
        low_weight = weights.astype(jnp.bfloat16).astype(jnp.float32)
        result = jnp.einsum("kgts,skd->kgtd", low_weight, value_blk, precision=lax.Precision.HIGHEST) / total[..., None]
        return result.transpose(2, 0, 1, 3).reshape(TOK_DEV, QH * HD)

    blocks = lax.map(one_block, jnp.arange(N_CTX, dtype=jnp.int32))
    attended = blocks.reshape(TOKENS, QH * HD).astype(jnp.bfloat16)
    return jnp.dot(attended, out_weight, preferred_element_type=jnp.float32).astype(jnp.bfloat16)
```

```python
import functools

import jax
import jax.numpy as jnp
from jax import lax
from jax.experimental import pallas as pl
from jax.experimental.pallas import tpu as pltpu
from jax.sharding import PartitionSpec as P

HD = 128
GROUP = 4
LONGEST = 4096
SHORT = 1024
CORES = 2
NEG_FILL = -1e30
POS_FILL = 1e30
SCALE = HD ** -0.5 * 1.4426950408889634
MESH = pl.DeviceIdType.MESH
PIECES = 2


def wide(x, count):
    return jnp.concatenate([x] * count, axis=1)


def kernel(
    n_ctx, n_head, n_slots, chunk,
    q_hbm, k_hbm, v_hbm, doc_ref, w_hbm, out_ref,
    q_ref, own, sib, slots, w_ref, acc, top, att, outbox, inbox,
    load_sem, send_sem, recv_sem, psend_sem, precv_sem,
):
    me = lax.axis_index("ctx")
    head = lax.axis_index("head")
    chip, core = me // CORES, lax.rem(me, CORES)
    chips = n_ctx // CORES
    side = lax.rem(chip, 2)
    sibling = chip * CORES + (1 - core)
    beside = (chip + 1 - 2 * side) * CORES + core
    ahead = me + 2 * CORES
    behind = me - 2 * CORES
    rows = q_ref.shape[0]
    q_heads = q_ref.shape[1] // HD
    part = rows // n_head
    width = w_ref.shape[1]

    loads = [
        pltpu.make_async_copy(src, dst, load_sem.at[n])
        for n, (src, dst) in enumerate(
            [(q_hbm, q_ref), (k_hbm, own.at[0]), (v_hbm, own.at[1]), (w_hbm, w_ref)]
        )
    ]
    for load in loads:
        load.start()

    barrier = pltpu.get_barrier_semaphore()
    has_ahead = chip + 2 < chips
    has_behind = chip >= 2

    def greet(target):
        pl.semaphore_signal(barrier, inc=1, device_id=target, device_id_type=MESH)

    greet({"ctx": sibling})
    greet({"ctx": beside})
    pl.when(has_ahead)(lambda: greet({"ctx": ahead}))
    pl.when(has_behind)(lambda: greet({"ctx": behind}))
    for d in range(1, n_head):
        greet({"head": lax.rem(head + d, n_head)})
    pl.semaphore_wait(
        barrier, n_head + 1 + has_ahead.astype(jnp.int32) + has_behind.astype(jnp.int32)
    )

    def arrive(k, half):
        return (k - 1) * CORES + half + 1

    def send(which, piece, src, dst, index, target):
        return pltpu.make_async_remote_copy(
            src_ref=src, dst_ref=dst,
            send_sem=send_sem.at[which, piece], recv_sem=recv_sem.at[index, piece],
            device_id={"ctx": target}, device_id_type=MESH,
        )

    def slot(k, half, piece):
        return slots.at[k - 1, piece, half]

    def received(k, half, piece):
        place = slot(k, half, piece)
        send(0, piece, place, place, arrive(k, half), sibling).wait_recv()

    sends = []

    def plan(which, src, dst, index, target, cond):
        copies = [send(which, t, src(t), dst(t), index, target) for t in range(PIECES)]
        sends.append((copies, cond))
        return copies

    own_src = lambda t: (k_hbm, v_hbm)[t]
    to_sib = plan(0, own_src, lambda t: sib.at[t], 0, sibling, core == 0)
    to_ahead = plan(1, own_src, lambda t: slot(2, core, t), arrive(2, core), ahead, has_ahead)
    to_side = plan(2, own_src, lambda t: slot(1, core, t), arrive(1, core), beside, side == 0)
    mine2 = lambda t: slot(2, core, t)
    mine1 = lambda t: slot(1, core, t)
    mine3 = lambda t: slot(3, core, t)
    side2even = plan(
        3, mine2, lambda t: slot(3, core, t), arrive(3, core), beside, has_behind & (side == 0)
    )
    side2odd = plan(
        4, mine2, lambda t: slot(1, core, t), arrive(1, core), beside, has_behind & (side == 1)
    )
    sib2 = plan(5, mine2, mine2, arrive(2, core), sibling, has_behind)
    sib1 = plan(6, mine1, mine1, arrive(1, core), sibling, chip >= 1)
    ahead1 = plan(
        7, mine1, lambda t: slot(3, core, t), arrive(3, core), ahead,
        has_behind & (side == 0) & has_ahead,
    )
    sib3 = plan(8, mine3, mine3, arrive(3, core), sibling, chip >= 3)
    conds = {id(c): cond for c, cond in sends}

    def go(copies, t):
        pl.when(conds[id(copies)])(lambda: copies[t].start())

    for t in range(PIECES):
        go(to_sib, t)
        go(to_ahead, t)
        go(to_side, t)

    if part % 128 == 0:
        groups = [(lax.rem(head + d, n_head) * part, part, [d]) for d in range(1, n_head)]
        groups.append((head * part, part, [0]))
    else:
        groups = [(0, rows, list(range(1, n_head)) + [0])]

    def attend(group, get_k, get_v, keys, first, element_mask, row_mask):
        start, count, _ = group
        row = pl.ds(pl.multiple_of(start, 64), count)

        def one(h, carry):
            kv = h // GROUP
            cols = pl.ds(pl.multiple_of(h * HD, HD), HD)
            kv_cols = pl.ds(pl.multiple_of(kv * HD, HD), HD)
            q = q_ref[row, cols]
            s = lax.dot_general(
                q, get_k(kv_cols), (((1,), (1,)), ((), ())), preferred_element_type=jnp.float32
            )
            if element_mask is not None:
                s = jnp.where(element_mask(), s, NEG_FILL)
            peak = jnp.broadcast_to(jnp.max(s, axis=1, keepdims=True), (count, HD))
            if row_mask is not None:
                seen = jnp.broadcast_to(row_mask(), (count, HD))
                peak = jnp.where(seen, peak, NEG_FILL)
            if not first:
                before = top[h, row, :]
                peak = jnp.maximum(before, peak)
            top[h, row, :] = peak
            base = peak
            if row_mask is not None:
                base = jnp.where(seen, peak, POS_FILL)
            p = jnp.exp2(s * SCALE - wide(base * SCALE, keys // HD)).astype(jnp.bfloat16)
            v = get_v(kv_cols)
            v = jnp.concatenate([v, jnp.ones_like(v)], axis=1)
            o = jnp.dot(p, v, preferred_element_type=jnp.float32)
            if not first:
                shrink = jnp.exp2((before - peak) * SCALE)
                o = o + acc[h, row, :] * wide(shrink, 2)
            acc[h, row, :] = o
            return carry

        lax.fori_loop(0, q_heads, one, 0)

    def own_mask(group):
        start, count, _ = group

        def mask():
            i = start + lax.broadcasted_iota(jnp.int32, (count, rows), 0)
            j = lax.broadcasted_iota(jnp.int32, (count, rows), 1)
            doc = doc_ref[pl.ds(pl.multiple_of(start, 64), count), :] - me * rows
            return (j <= i) & (j >= doc)

        return mask

    def sib_mask(group):
        start, count, _ = group

        def mask():
            j = lax.broadcasted_iota(jnp.int32, (count, rows), 1)
            doc = doc_ref[pl.ds(pl.multiple_of(start, 64), count), :] - sibling * rows
            return j >= doc

        return mask

    def slot_mask(group, k):
        start, count, _ = group
        return lambda: doc_ref[pl.ds(pl.multiple_of(start, 64), count), :] <= (chip - k) * CORES * rows

    def attend_slot(group, k):
        def run():
            keys = CORES * rows
            attend(
                group,
                lambda c: slots[k - 1, 0, :, :, c].reshape(keys, HD),
                lambda c: slots[k - 1, 1, :, :, c].reshape(keys, HD),
                keys, False, None, slot_mask(group, k),
            )

        pl.when(chip >= k)(run)

    loads[0].wait()
    loads[1].wait()
    loads[2].wait()
    for group in groups:
        attend(
            group, lambda c: own[0, :, c], lambda c: own[1, :, c], rows, True, own_mask(group), None
        )

    @pl.when(core == 1)
    def _():
        for t in range(PIECES):
            send(0, t, sib.at[t], sib.at[t], 0, sibling).wait_recv()
        for group in groups:
            attend(
                group, lambda c: sib[0, :, c], lambda c: sib[1, :, c], rows, False,
                sib_mask(group), None,
            )

    def relay(k, onward):
        @pl.when(chip >= k)
        def _():
            for t in range(PIECES):
                received(k, core, t)
                for copies in onward:
                    go(copies, t)

    def complete(k):
        @pl.when(chip >= k)
        def _():
            for t in range(PIECES):
                received(k, 1 - core, t)

    relay(2, [side2even, side2odd, sib2])
    relay(1, [ahead1, sib1])
    complete(2)
    for group in groups:
        attend_slot(group, 2)
    relay(3, [sib3])
    complete(1)
    for group in groups:
        attend_slot(group, 1)
    complete(3)
    loads[3].wait()

    pieces = width // chunk

    def parcel(d, n):
        cols = pl.ds(n * chunk, chunk)
        return pltpu.make_async_remote_copy(
            src_ref=outbox.at[d - 1, :, cols], dst_ref=inbox.at[d - 1, :, cols],
            send_sem=psend_sem.at[d - 1, n], recv_sem=precv_sem.at[d - 1, n],
            device_id={"head": lax.rem(head + d, n_head)}, device_id_type=MESH,
        )

    for group in groups:
        attend_slot(group, 3)
        start, count, dests = group
        row = pl.ds(pl.multiple_of(start, 64), count)

        def finish(h, carry):
            cols = pl.ds(pl.multiple_of(h * HD, HD), HD)
            att[row, cols] = (acc[h, row, :HD] / acc[h, row, HD:]).astype(jnp.bfloat16)
            return carry

        lax.fori_loop(0, q_heads, finish, 0)
        for d in dests:
            dest_row = pl.ds(pl.multiple_of(lax.rem(head + d, n_head) * part, 64), part)
            for n in range(pieces):
                cols = pl.ds(n * chunk, chunk)
                total = jnp.dot(
                    att[dest_row, :], w_ref[:, cols], preferred_element_type=jnp.float32
                )
                if d:
                    outbox[d - 1, :, cols] = total.astype(jnp.bfloat16)
                    parcel(d, n).start()
                else:
                    for e in range(1, n_head):
                        parcel(e, n).wait_recv()
                        total = total + inbox[e - 1, :, cols].astype(jnp.float32)
                    out_ref[:, cols] = total.astype(jnp.bfloat16)

    for copies, cond in sends:
        @pl.when(cond)
        def _(copies=copies):
            for copy in copies:
                copy.wait_send()
    for d in range(1, n_head):
        for n in range(pieces):
            parcel(d, n).wait_send()


def on_device(n_ctx, n_head, queries, keys, values, doc_start, out_weight):
    rows, q_width = queries.shape
    kv_width = keys.shape[1]
    width = out_weight.shape[1]
    part = rows // n_head
    q_heads = q_width // HD
    n_slots = LONGEST // SHORT - 1
    chunk = 512
    bf16, f32 = jnp.bfloat16, jnp.float32
    anywhere = pl.BlockSpec(memory_space=pl.ANY)
    vmem = pl.BlockSpec(memory_space=pltpu.VMEM)
    peers = max(n_head - 1, 1)
    return pl.pallas_call(
        functools.partial(kernel, n_ctx, n_head, n_slots, chunk),
        out_shape=jax.ShapeDtypeStruct((part, width), bf16),
        in_specs=[anywhere, anywhere, anywhere, vmem, anywhere],
        out_specs=vmem,
        scratch_shapes=[
            pltpu.VMEM((rows, q_width), bf16),
            pltpu.VMEM((2, rows, kv_width), bf16),
            pltpu.VMEM((2, rows, kv_width), bf16),
            pltpu.VMEM((n_slots, 2, CORES, rows, kv_width), bf16),
            pltpu.VMEM((q_width, width), bf16),
            pltpu.VMEM((q_heads, rows, 2 * HD), f32),
            pltpu.VMEM((q_heads, rows, HD), f32),
            pltpu.VMEM((rows, q_width), bf16),
            pltpu.VMEM((peers, part, width), bf16),
            pltpu.VMEM((peers, part, width), bf16),
            pltpu.SemaphoreType.DMA((4,)),
            pltpu.SemaphoreType.DMA((9, PIECES)),
            pltpu.SemaphoreType.DMA((1 + n_slots * CORES, PIECES)),
            pltpu.SemaphoreType.DMA((peers, width // chunk)),
            pltpu.SemaphoreType.DMA((peers, width // chunk)),
        ],
        compiler_params=pltpu.CompilerParams(
            collective_id=0, has_side_effects=True, vmem_limit_bytes=60 * 1024 * 1024
        ),
    )(queries, keys, values, doc_start.reshape(rows, 1), out_weight)


def solution(mesh):
    return jax.shard_map(
        functools.partial(on_device, mesh.shape["ctx"], mesh.shape["head"]),
        mesh=mesh,
        in_specs=(P("ctx", "head"), P("ctx", "head"), P("ctx", "head"), P("ctx"), P("head", None)),
        out_specs=P(("ctx", "head"), None),
        check_vma=False,
    )
```

```python
import functools

import jax
import jax.numpy as jnp
from jax import lax
from jax.experimental import pallas as pl
from jax.experimental.pallas import tpu as pltpu
from jax.sharding import PartitionSpec as P

HD = 128
GROUP = 4
LONGEST = 4096
SHORT = 1024
CORES = 2
NEG_FILL = -1e30
POS_FILL = 1e30
SCALE = HD ** -0.5 * 1.4426950408889634
MESH = pl.DeviceIdType.MESH
PIECES = 4
HALVES = PIECES // 2


def wide(x, count):
    return jnp.concatenate([x] * count, axis=1)


def kernel(
    n_ctx, n_head, n_slots, chunk,
    q_hbm, k_hbm, v_hbm, doc_ref, w_hbm, out_ref,
    q_ref, own, sib, slots, w_ref, acc, top, att, outbox, inbox,
    load_sem, send_sem, recv_sem, psend_sem, precv_sem,
):
    me = lax.axis_index("ctx")
    head = lax.axis_index("head")
    chip, core = me // CORES, lax.rem(me, CORES)
    chips = n_ctx // CORES
    side = lax.rem(chip, 2)
    sibling = chip * CORES + (1 - core)
    beside = (chip + 1 - 2 * side) * CORES + core
    ahead = me + 2 * CORES
    behind = me - 2 * CORES
    rows = q_ref.shape[0]
    q_heads = q_ref.shape[1] // HD
    part = rows // n_head
    width = w_ref.shape[1]

    loads = [
        pltpu.make_async_copy(src, dst, load_sem.at[n])
        for n, (src, dst) in enumerate(
            [(q_hbm, q_ref), (k_hbm, own.at[0]), (v_hbm, own.at[1]), (w_hbm, w_ref)]
        )
    ]
    for load in loads:
        load.start()

    barrier = pltpu.get_barrier_semaphore()
    has_ahead = chip + 2 < chips
    has_behind = chip >= 2

    def greet(target):
        pl.semaphore_signal(barrier, inc=1, device_id=target, device_id_type=MESH)

    greet({"ctx": sibling})
    greet({"ctx": beside})
    pl.when(has_ahead)(lambda: greet({"ctx": ahead}))
    pl.when(has_behind)(lambda: greet({"ctx": behind}))
    for d in range(1, n_head):
        greet({"head": lax.rem(head + d, n_head)})
    pl.semaphore_wait(
        barrier, n_head + 1 + has_ahead.astype(jnp.int32) + has_behind.astype(jnp.int32)
    )

    span = rows // HALVES

    def stretch(piece):
        return pl.ds(piece % HALVES * span, span)

    def arrive(k, half):
        return (k - 1) * CORES + half + 1

    def send(which, piece, src, dst, index, target):
        return pltpu.make_async_remote_copy(
            src_ref=src, dst_ref=dst,
            send_sem=send_sem.at[which, piece], recv_sem=recv_sem.at[index, piece],
            device_id={"ctx": target}, device_id_type=MESH,
        )

    def slot(k, half, piece):
        return slots.at[k - 1, piece // HALVES, half, stretch(piece), :]

    def received(k, half, piece):
        place = slot(k, half, piece)
        send(0, piece, place, place, arrive(k, half), sibling).wait_recv()

    sends = []

    def plan(which, src, dst, index, target, cond):
        copies = [send(which, t, src(t), dst(t), index, target) for t in range(PIECES)]
        sends.append((copies, cond))
        return copies

    own_src = lambda t: (k_hbm, v_hbm)[t // HALVES].at[stretch(t), :]
    in_sib = lambda t: sib.at[t // HALVES, stretch(t), :]
    to_sib = plan(0, own_src, in_sib, 0, sibling, core == 0)
    to_ahead = plan(1, own_src, lambda t: slot(2, core, t), arrive(2, core), ahead, has_ahead)
    to_side = plan(2, own_src, lambda t: slot(1, core, t), arrive(1, core), beside, side == 0)
    mine2 = lambda t: slot(2, core, t)
    mine1 = lambda t: slot(1, core, t)
    mine3 = lambda t: slot(3, core, t)
    side2even = plan(
        3, mine2, lambda t: slot(3, core, t), arrive(3, core), beside, has_behind & (side == 0)
    )
    side2odd = plan(
        4, mine2, lambda t: slot(1, core, t), arrive(1, core), beside, has_behind & (side == 1)
    )
    sib2 = plan(5, mine2, mine2, arrive(2, core), sibling, has_behind)
    sib1 = plan(6, mine1, mine1, arrive(1, core), sibling, chip >= 1)
    ahead1 = plan(
        7, mine1, lambda t: slot(3, core, t), arrive(3, core), ahead,
        has_behind & (side == 0) & has_ahead,
    )
    sib3 = plan(8, mine3, mine3, arrive(3, core), sibling, chip >= 3)
    conds = {id(c): cond for c, cond in sends}

    def go(copies, t):
        pl.when(conds[id(copies)])(lambda: copies[t].start())

    for t in range(PIECES):
        go(to_sib, t)
        go(to_ahead, t)
        go(to_side, t)

    if part % 128 == 0:
        groups = [(lax.rem(head + d, n_head) * part, part, [d]) for d in range(1, n_head)]
        groups.append((head * part, part, [0]))
    else:
        groups = [(0, rows, list(range(1, n_head)) + [0])]

    def attend(group, get_k, get_v, keys, first, element_mask, row_mask):
        start, count, _ = group
        row = pl.ds(pl.multiple_of(start, 64), count)

        def one(h, carry):
            kv = h // GROUP
            cols = pl.ds(pl.multiple_of(h * HD, HD), HD)
            kv_cols = pl.ds(pl.multiple_of(kv * HD, HD), HD)
            q = q_ref[row, cols]
            s = lax.dot_general(
                q, get_k(kv_cols), (((1,), (1,)), ((), ())), preferred_element_type=jnp.float32
            )
            if element_mask is not None:
                s = jnp.where(element_mask(), s, NEG_FILL)
            peak = jnp.broadcast_to(jnp.max(s, axis=1, keepdims=True), (count, HD))
            if row_mask is not None:
                seen = jnp.broadcast_to(row_mask(), (count, HD))
                peak = jnp.where(seen, peak, NEG_FILL)
            if not first:
                before = top[h, row, :]
                peak = jnp.maximum(before, peak)
            top[h, row, :] = peak
            base = peak
            if row_mask is not None:
                base = jnp.where(seen, peak, POS_FILL)
            p = jnp.exp2(s * SCALE - wide(base * SCALE, keys // HD)).astype(jnp.bfloat16)
            v = get_v(kv_cols)
            v = jnp.concatenate([v, jnp.ones_like(v)], axis=1)
            o = jnp.dot(p, v, preferred_element_type=jnp.float32)
            if not first:
                shrink = jnp.exp2((before - peak) * SCALE)
                o = o + acc[h, row, :] * wide(shrink, 2)
            acc[h, row, :] = o
            return carry

        lax.fori_loop(0, q_heads, one, 0, unroll=4)

    def own_mask(group):
        start, count, _ = group

        def mask():
            i = start + lax.broadcasted_iota(jnp.int32, (count, rows), 0)
            j = lax.broadcasted_iota(jnp.int32, (count, rows), 1)
            doc = doc_ref[pl.ds(pl.multiple_of(start, 64), count), :] - me * rows
            return (j <= i) & (j >= doc)

        return mask

    def sib_mask(group):
        start, count, _ = group

        def mask():
            j = lax.broadcasted_iota(jnp.int32, (count, rows), 1)
            doc = doc_ref[pl.ds(pl.multiple_of(start, 64), count), :] - sibling * rows
            return j >= doc

        return mask

    def slot_mask(group, k):
        start, count, _ = group
        return lambda: doc_ref[pl.ds(pl.multiple_of(start, 64), count), :] <= (chip - k) * CORES * rows

    def attend_slot(group, k):
        def run():
            keys = CORES * rows
            attend(
                group,
                lambda c: slots[k - 1, 0, :, :, c].reshape(keys, HD),
                lambda c: slots[k - 1, 1, :, :, c].reshape(keys, HD),
                keys, False, None, slot_mask(group, k),
            )

        pl.when(chip >= k)(run)

    def relay(k, t):
        onward = {1: [ahead1, sib1], 2: [side2even, side2odd, sib2], 3: [sib3]}[k]

        @pl.when(chip >= k)
        def _():
            received(k, core, t)
            for copies in onward:
                go(copies, t)

    def complete(k):
        @pl.when(chip >= k)
        def _():
            for t in range(PIECES):
                received(k, 1 - core, t)

    def attend_own(group):
        attend(
            group, lambda c: own[0, :, c], lambda c: own[1, :, c], rows, True, own_mask(group), None
        )

    def attend_sib(group):
        pl.when(core == 1)(lambda: attend(
            group, lambda c: sib[0, :, c], lambda c: sib[1, :, c], rows, False,
            sib_mask(group), None,
        ))

    early, late = groups[:-1], groups[-1:]
    loads[0].wait()
    loads[1].wait()
    loads[2].wait()
    for group in groups:
        attend_own(group)
    relay(2, 0)
    relay(2, 1)

    @pl.when(core == 1)
    def _():
        for t in range(PIECES):
            send(0, t, in_sib(t), in_sib(t), 0, sibling).wait_recv()

    for group in early:
        attend_sib(group)
    relay(1, 0)
    relay(2, 2)
    for group in late:
        attend_sib(group)
    relay(1, 1)
    relay(2, 3)
    complete(2)
    for group in early:
        attend_slot(group, 2)
    relay(1, 2)
    relay(1, 3)
    relay(3, 0)
    relay(3, 1)
    complete(1)
    for group in early:
        attend_slot(group, 1)
    relay(3, 2)
    relay(3, 3)
    complete(3)
    loads[3].wait()

    pieces = width // chunk

    def parcel(d, n):
        cols = pl.ds(n * chunk, chunk)
        return pltpu.make_async_remote_copy(
            src_ref=outbox.at[d - 1, :, cols], dst_ref=inbox.at[d - 1, :, cols],
            send_sem=psend_sem.at[d - 1, n], recv_sem=precv_sem.at[d - 1, n],
            device_id={"head": lax.rem(head + d, n_head)}, device_id_type=MESH,
        )

    for group in groups:
        if group is groups[-1]:
            attend_slot(group, 2)
            attend_slot(group, 1)
        attend_slot(group, 3)
        start, count, dests = group
        row = pl.ds(pl.multiple_of(start, 64), count)

        def finish(h, carry):
            cols = pl.ds(pl.multiple_of(h * HD, HD), HD)
            att[row, cols] = (acc[h, row, :HD] / acc[h, row, HD:]).astype(jnp.bfloat16)
            return carry

        lax.fori_loop(0, q_heads, finish, 0)
        for d in dests:
            dest_row = pl.ds(pl.multiple_of(lax.rem(head + d, n_head) * part, 64), part)
            for n in range(pieces):
                cols = pl.ds(n * chunk, chunk)
                total = jnp.dot(
                    att[dest_row, :], w_ref[:, cols], preferred_element_type=jnp.float32
                )
                if d:
                    outbox[d - 1, :, cols] = total.astype(jnp.bfloat16)
                    parcel(d, n).start()
                else:
                    for e in range(1, n_head):
                        parcel(e, n).wait_recv()
                        total = total + inbox[e - 1, :, cols].astype(jnp.float32)
                    out_ref[:, cols] = total.astype(jnp.bfloat16)

    for copies, cond in sends:
        @pl.when(cond)
        def _(copies=copies):
            for copy in copies:
                copy.wait_send()
    for d in range(1, n_head):
        for n in range(pieces):
            parcel(d, n).wait_send()


def on_device(n_ctx, n_head, queries, keys, values, doc_start, out_weight):
    rows, q_width = queries.shape
    kv_width = keys.shape[1]
    width = out_weight.shape[1]
    part = rows // n_head
    q_heads = q_width // HD
    n_slots = LONGEST // SHORT - 1
    chunk = 512
    bf16, f32 = jnp.bfloat16, jnp.float32
    anywhere = pl.BlockSpec(memory_space=pl.ANY)
    vmem = pl.BlockSpec(memory_space=pltpu.VMEM)
    peers = max(n_head - 1, 1)
    return pl.pallas_call(
        functools.partial(kernel, n_ctx, n_head, n_slots, chunk),
        out_shape=jax.ShapeDtypeStruct((part, width), bf16),
        in_specs=[anywhere, anywhere, anywhere, vmem, anywhere],
        out_specs=vmem,
        scratch_shapes=[
            pltpu.VMEM((rows, q_width), bf16),
            pltpu.VMEM((2, rows, kv_width), bf16),
            pltpu.VMEM((2, rows, kv_width), bf16),
            pltpu.VMEM((n_slots, 2, CORES, rows, kv_width), bf16),
            pltpu.VMEM((q_width, width), bf16),
            pltpu.VMEM((q_heads, rows, 2 * HD), f32),
            pltpu.VMEM((q_heads, rows, HD), f32),
            pltpu.VMEM((rows, q_width), bf16),
            pltpu.VMEM((peers, part, width), bf16),
            pltpu.VMEM((peers, part, width), bf16),
            pltpu.SemaphoreType.DMA((4,)),
            pltpu.SemaphoreType.DMA((9, PIECES)),
            pltpu.SemaphoreType.DMA((1 + n_slots * CORES, PIECES)),
            pltpu.SemaphoreType.DMA((peers, width // chunk)),
            pltpu.SemaphoreType.DMA((peers, width // chunk)),
        ],
        compiler_params=pltpu.CompilerParams(
            collective_id=0, has_side_effects=True, vmem_limit_bytes=60 * 1024 * 1024
        ),
    )(queries, keys, values, doc_start.reshape(rows, 1), out_weight)


def solution(mesh):
    return jax.shard_map(
        functools.partial(on_device, mesh.shape["ctx"], mesh.shape["head"]),
        mesh=mesh,
        in_specs=(P("ctx", "head"), P("ctx", "head"), P("ctx", "head"), P("ctx"), P("head", None)),
        out_specs=P(("ctx", "head"), None),
        check_vma=False,
    )
```
